256 devices in a mesh: seq: 2 (over y_lo), row: 16 (over z, core), col: 8 (over x, y_hi).
Axes of the slice: x: 4, y: 4 (y_hi: 2, y_lo: 2; y = y_hi * 2 + y_lo), z: 8, core: 2. Of those that a mesh axis runs over, the one named last changes fastest.
Arguments:
- hidden: bfloat16 [4096, 5120], P('seq', 'row'), may hold values from -6 to 6
- w_query: bfloat16 [5120, 4096], P('row', 'col'), may hold values from -0.5031153 to 0.5031153
- w_key: bfloat16 [5120, 1024], P('row', 'col'), may hold values from -0.5031153 to 0.5031153
- w_value: bfloat16 [5120, 1024], P('row', 'col'), may hold values from -0.078125 to 0.078125
- w_ssm_in: bfloat16 [5120, 4096], P('row', 'col'), may hold values from -0.078125 to 0.078125
- w_gate: bfloat16 [5120, 4096], P('row', 'col'), may hold values from -0.078125 to 0.078125
- w_bc: bfloat16 [5120, 256], P('row'), may hold values from -0.078125 to 0.078125
- w_dt: bfloat16 [5120, 64], P('row', 'col'), may hold values from -0.078125 to 0.078125
- dt_bias: float32 [64], P('col'), may hold values from -2 to 0.5
- a_rate: float32 [64], P('col'), may hold values from 0.00012207031 to 0.04
- d_skip: float32 [64], P('col'), may hold values from 0.5 to 1.5
- w_attn_out: bfloat16 [4096, 5120], P('col', 'row'), may hold values from -0.09375 to 0.09375
- w_ssm_out: bfloat16 [4096, 5120], P('col', 'row'), may hold values from -0.09375 to 0.09375
Outputs:
- mixed: bfloat16 [4096, 5120], P(('seq', 'col'), 'row')
The draws below stay inside these ranges and needn't reach their ends.
All inputs are finite; a program needn't handle non-finite values.
Results may differ from the reference program's by a relative error of at most 0.017.
The reference program's roundings to bfloat16 on the way (of `ssm_out` and `attn_out`) count: a program that leaves them out, or rounds other values in their place, can miss the bound.
Values may be sent and summed in bfloat16 or wider, within the bound.
No kernel may reach another device: no remote copies, remote signals or barrier semaphores. Data moves between devices by JAX's collectives and lax.ppermute only.
A program may use at most 128 MiB of HBM per device.

```python
import math
import jax
import jax.numpy as jnp
from jax import lax

D = 5120
HQ = 32
KVH = 8
HD = 128
SH = 64
HP = 64
NSTATE = 128
TOK_DEV = 128
TOKENS = 4096


def scaled_normal(key, shape, spread):
    values = jax.random.normal(key, shape, jnp.float32)
    return (jnp.clip(values, -6.0, 6.0) * (spread / math.sqrt(D))).astype(jnp.bfloat16)


def draw_w_query(key, part):
    key = jax.random.fold_in(key, 11)
    spread = 1.0
    return scaled_normal(key, (D, HQ * HD), spread)


def draw_w_key(key, part):
    key = jax.random.fold_in(key, 12)
    spread = 1.0
    return scaled_normal(key, (D, KVH * HD), spread)


def block_scale(rng, dims, pieces, low, high):
    def one(axis_at, blocks):
        heights = jax.random.uniform(jax.random.fold_in(jax.random.fold_in(rng, 6), axis_at), (blocks,), jnp.float32, low / len(pieces), high / len(pieces))
        return jnp.repeat(jnp.exp(heights), dims[axis_at] // blocks).reshape((-1,) + (1,) * (len(dims) - axis_at - 1))

    gain = one(*pieces[0])
    for cut in pieces[1:]:
        gain = gain * one(*cut)
    return gain


def gaussian(stream_key, dims, scale, most, split=(), held_as=jnp.bfloat16):
    loudness = block_scale(stream_key, dims, split, -0.22, 0.18) if split else 1.0
    entries = jax.random.normal(stream_key, dims, jnp.float32) * scale * loudness
    return jnp.minimum(jnp.maximum(entries, -most), most).astype(held_as)


def setup_inputs(seed: int = 0) -> dict:
    streams_of = jax.random.split(jax.random.key(seed), 14)
    hidden = gaussian(streams_of[0], (TOKENS, D), 1.0, 6.0, ((0, 2), (1, 16)))
    w_query = draw_w_query(jax.random.fold_in(streams_of[13], 71), 0)
    w_key = draw_w_key(jax.random.fold_in(streams_of[13], 71), 0)
    w_value = gaussian(streams_of[3], (D, KVH * HD), D ** -0.5, 0.078125, ((0, 16), (1, 8)))
    w_ssm_in = gaussian(streams_of[4], (D, SH * HP), D ** -0.5, 0.078125, ((0, 16), (1, 8)))
    w_gate = gaussian(streams_of[5], (D, SH * HP), D ** -0.5, 0.078125, ((0, 16), (1, 8)))
    w_bc = gaussian(streams_of[6], (D, 2 * NSTATE), D ** -0.5, 0.078125, ((0, 16),))
    w_dt = gaussian(streams_of[7], (D, SH), D ** -0.5, 0.078125, ((0, 16), (1, 8)))
    dt_bias = jnp.clip(-2.0 + 2.5 * jax.random.uniform(streams_of[8], (SH,), jnp.float32) ** block_scale(streams_of[8], (SH,), ((0, 8),), -0.2, 0.2), -2.0, 0.5)
    a_rate = jnp.clip(jnp.exp(math.log(0.04) - 5.7920375 * jax.random.uniform(streams_of[9], (SH,), jnp.float32) ** block_scale(streams_of[9], (SH,), ((0, 8),), -0.2, 0.2)), 0.00012207031, 0.04)
    d_skip = jnp.clip(0.5 + 1.0 * jax.random.uniform(streams_of[10], (SH,), jnp.float32) ** block_scale(streams_of[10], (SH,), ((0, 8),), -0.2, 0.2), 0.5, 1.5)
    w_attn_out = gaussian(streams_of[11], (HQ * HD, D), (HQ * HD) ** -0.5, 0.09375, ((0, 8), (1, 16)))
    w_ssm_out = gaussian(streams_of[12], (SH * HP, D), (SH * HP) ** -0.5, 0.09375, ((0, 8), (1, 16)))
    return {"hidden": hidden, "w_query": w_query, "w_key": w_key, "w_value": w_value, "w_ssm_in": w_ssm_in, "w_gate": w_gate, "w_bc": w_bc, "w_dt": w_dt, "dt_bias": dt_bias, "a_rate": a_rate, "d_skip": d_skip, "w_attn_out": w_attn_out, "w_ssm_out": w_ssm_out}


def attention_all(query, keys, values):
    group = HQ // KVH
    highest = lax.Precision.HIGHEST
    grouped = query.astype(jnp.float32).reshape(TOKENS, KVH, group, HD)
    key_all = keys.astype(jnp.float32).reshape(TOKENS, KVH, HD)
    value_all = values.astype(jnp.float32).reshape(TOKENS, KVH, HD)
    block = math.gcd(TOKENS, 512)
    position = jnp.arange(TOKENS, dtype=jnp.int32)
    scale = HD ** (-0.5)

    def one_block(start):
        rows = lax.dynamic_slice_in_dim(grouped, start, block, 0)
        query_pos = start + jnp.arange(block, dtype=jnp.int32)
        scores = jnp.einsum('tkgd,mkd->kgtm', rows, key_all, precision=highest) * scale
        valid = position[None, :] <= query_pos[:, None]
        scores = jnp.where(valid, scores, -jnp.inf)
        best = lax.optimization_barrier(jnp.max(scores, axis=-1, keepdims=True))
        weights = jnp.exp(scores - best)
        total = lax.optimization_barrier(jnp.sum(weights, axis=-1))
        summed = jnp.einsum('kgtm,mkd->kgtd', weights, value_all, precision=highest)
        output = summed / total[..., None]
        return output.transpose(2, 0, 1, 3).reshape(block, HQ * HD)
    starts = jnp.arange(0, TOKENS, block, dtype=jnp.int32)
    return lax.map(one_block, starts).reshape(TOKENS, HQ * HD).astype(jnp.bfloat16)

def ssd_all(ssm_raw, gate_raw, bc_raw, dt_raw, dt_bias, a_rate, d_skip):
    blocks = TOKENS // TOK_DEV
    highest = lax.Precision.HIGHEST

    def blocked(array):
        return array.reshape(blocks, TOK_DEV, array.shape[1])

    def one_block(state, inputs_all):
        ssm_part, gate_part, bc_part, dt_part = inputs_all
        inputs = jax.nn.silu(ssm_part).reshape(TOK_DEV, SH, HP)
        gates = gate_part.reshape(TOK_DEV, SH, HP)
        bc_act = jax.nn.silu(bc_part)
        b_rows = bc_act[:, :NSTATE]
        c_rows = bc_act[:, NSTATE:]
        step_size = jax.nn.softplus(dt_part + dt_bias[None, :])
        cumulative = jnp.cumsum(-a_rate[None, :] * step_size, axis=0)
        position = jnp.arange(TOK_DEV)
        lower = position[:, None] >= position[None, :]
        inner = jnp.dot(c_rows, b_rows.T, precision=highest)
        decays = jnp.exp(jnp.where(lower[:, :, None], cumulative[:, None, :] - cumulative[None, :, :], -jnp.inf))
        coefficient = inner[:, :, None] * decays * step_size[None, :, :]
        within = jnp.einsum('tuh,uhp->thp', coefficient, inputs, precision=highest)
        to_end = jnp.exp(cumulative[-1][None, :] - cumulative) * step_size
        local_state = jnp.einsum('uh,uhp,un->hpn', to_end, inputs, b_rows, precision=highest)
        block_decay = jnp.exp(cumulative[-1])
        carried = jnp.exp(cumulative)[:, :, None] * jnp.einsum('hpn,tn->thp', state, c_rows, precision=highest)
        result = within + carried + d_skip[None, :, None] * inputs
        gated = result * jax.nn.silu(gates)
        normed = gated * lax.rsqrt(lax.optimization_barrier(jnp.mean(gated * gated, axis=-1, keepdims=True)) + 1e-05)
        new_state = block_decay[:, None, None] * state + local_state
        return (new_state, normed.reshape(TOK_DEV, SH * HP).astype(jnp.bfloat16))
    initial = jnp.zeros((SH, HP, NSTATE), jnp.float32)
    final_state, outputs = lax.scan(one_block, initial, (blocked(ssm_raw), blocked(gate_raw), blocked(bc_raw), blocked(dt_raw)))
    return outputs.reshape(TOKENS, SH * HP)

def reference(hidden, w_query, w_key, w_value, w_ssm_in, w_gate, w_bc, w_dt, dt_bias, a_rate, d_skip, w_attn_out, w_ssm_out):

    def project(weight):
        return jnp.dot(hidden, weight, preferred_element_type=jnp.float32)
    query = project(w_query).astype(jnp.bfloat16)
    keys = project(w_key).astype(jnp.bfloat16)
    values = project(w_value).astype(jnp.bfloat16)
    attn_out = attention_all(query, keys, values)
    ssm_out = ssd_all(project(w_ssm_in), project(w_gate), project(w_bc), project(w_dt), dt_bias, a_rate, d_skip)
    mixed = jnp.dot(attn_out, w_attn_out, preferred_element_type=jnp.float32) + jnp.dot(ssm_out, w_ssm_out, preferred_element_type=jnp.float32)
    return mixed.astype(jnp.bfloat16)
```

```python
import jax
import jax.numpy as jnp
from jax import lax
from jax.sharding import PartitionSpec as P

HD = 128
HP = 64
NSTATE = 128
RING = 8
ROWS = 16
COLS = 8
F32 = jnp.float32
BF16 = jnp.bfloat16
HIGHEST = lax.Precision.HIGHEST


def ring_step(array, step):
    return lax.ppermute(array, "row", [(i, (i + 2 * step) % ROWS) for i in range(ROWS)])


def other_core(array):
    return lax.ppermute(array, "row", [(i, i ^ 1) for i in range(ROWS)])


def ring_reduce(partial, wire, right_hops):
    left_hops = RING - 1 - right_hops
    right = left = None
    for hop in range(max(right_hops, left_hops), 0, -1):
        if hop <= right_hops:
            term = partial(hop)
            right = ring_step((term if right is None else right.astype(F32) + term).astype(wire), 1)
        if hop <= left_hops:
            term = partial(-hop)
            left = ring_step((term if left is None else left.astype(F32) + term).astype(wire), -1)
    return partial(0) + right.astype(F32) + left.astype(F32)


def attention(query, query_start, keys, values, key_start):
    tok_rows = query.shape[1]
    group = query.shape[0] // HD
    query_pos = query_start + jnp.arange(tok_rows, dtype=jnp.int32)
    key_pos = (key_start[:, None] + jnp.arange(tok_rows, dtype=jnp.int32)[None, :]).reshape(-1)
    grouped = query.reshape(group, HD, tok_rows)
    scores = jnp.einsum("gdt,dm->gtm", grouped, keys, preferred_element_type=F32) * HD ** (-0.5)
    valid = key_pos[None, :] <= query_pos[:, None]
    scores = jnp.where(valid, scores, -1e30)
    best = jnp.max(scores, axis=-1, keepdims=True)
    weights = jnp.exp(scores - best).astype(BF16)
    total = jnp.sum(weights.astype(F32), axis=-1)
    summed = jnp.einsum("gtm,md->gtd", weights, values, preferred_element_type=F32)
    output = summed / total[..., None]
    return output.transpose(1, 0, 2).reshape(tok_rows, group * HD).astype(BF16)


def on_device(
    hidden,
    w_query,
    w_key,
    w_value,
    w_ssm_in,
    w_gate,
    w_bc,
    w_dt,
    dt_bias,
    a_rate,
    d_skip,
    w_attn_out,
    w_ssm_out,
):
    row = lax.axis_index("row")
    seq = lax.axis_index("seq")
    chip = row // 2
    core = row % 2
    half_rows = hidden.shape[0]
    tok_rows = half_rows // ROWS
    heads = w_dt.shape[1]
    head_rows = heads * HP
    query_width = w_query.shape[1]
    kv_width = w_value.shape[1]
    bc_width = w_bc.shape[1]
    ssm_width = w_ssm_in.shape[1]

    hidden_other = other_core(hidden)
    w_wide = jnp.concatenate([w_query, w_key, w_bc, w_dt], axis=1)
    w_narrow = jnp.concatenate([w_value, w_ssm_in, w_gate], axis=1)
    w_wide, w_narrow = (jnp.concatenate([w, other_core(w)], axis=0) for w in (w_wide, w_narrow))

    def block_of(hop):
        start = (((chip + hop + RING) % RING) * 2 + core) * tok_rows
        return jnp.concatenate(
            [lax.dynamic_slice_in_dim(h, start, tok_rows, 0) for h in (hidden, hidden_other)], axis=1
        )

    blocks = {hop: block_of(hop) for hop in range(1 - RING // 2, RING // 2 + 1)}
    blocks[-RING // 2] = blocks[RING // 2]

    def project_wide(hop):
        return lax.dot_general(w_wide, blocks[hop], (((0,), (1,)), ((), ())), preferred_element_type=F32)

    def project_narrow(hop):
        return jnp.dot(blocks[hop], w_narrow, preferred_element_type=F32)

    narrow = ring_reduce(project_narrow, BF16, 3)
    wide = ring_reduce(project_wide, F32, 4)

    query = wide[:query_width].astype(BF16)
    key = wide[query_width : query_width + kv_width].astype(BF16)
    bc_act = jax.nn.silu(wide[query_width + kv_width : query_width + kv_width + bc_width])
    dt_raw = wide[query_width + kv_width + bc_width :]
    value = narrow[:, :kv_width].astype(BF16)
    inputs = jax.nn.silu(narrow[:, kv_width : kv_width + ssm_width])
    gate_raw = narrow[:, kv_width + ssm_width :]

    b_cols = bc_act[:NSTATE]
    c_cols = bc_act[NSTATE:]
    step_size = jax.nn.softplus(dt_raw + dt_bias[:, None])
    position = jnp.arange(tok_rows)
    upto = (position[:, None] <= position[None, :]).astype(F32)
    cumulative = jnp.dot(-a_rate[:, None] * step_size, upto, precision=HIGHEST)
    to_end = jnp.exp(cumulative[:, -1:] - cumulative) * step_size

    def over_heads(per_head):
        return jnp.broadcast_to(per_head.T[:, :, None], (tok_rows, heads, HP)).reshape(tok_rows, head_rows)

    local = lax.dot_general(
        inputs * over_heads(to_end), b_cols, (((0,), (1,)), ((), ())), precision=HIGHEST
    )
    log_block = cumulative[:, -1]
    log_high = log_block.astype(BF16)
    log_low = (log_block - log_high.astype(F32)).astype(BF16)
    log_rows = jnp.broadcast_to(jnp.concatenate([log_high, log_low])[:, None], (2 * heads, NSTATE))
    pair = jnp.concatenate([key, value], axis=0)
    pair_other = lax.ppermute(pair, "seq", [(0, 1), (1, 0)])
    message = jnp.concatenate([pair, pair_other, local.astype(BF16), log_rows], axis=0)
    gathered = lax.all_gather(message, "row", axis=0, tiled=False)

    pairs = jnp.stack([gathered[:, : 2 * HD], gathered[:, 2 * HD : 4 * HD]])
    keys = pairs[:, :, :HD].transpose(2, 0, 1, 3).reshape(HD, -1)
    values = pairs[:, :, HD:].reshape(-1, HD)
    places = jnp.arange(ROWS, dtype=jnp.int32)
    key_start = jnp.concatenate([seq * half_rows + places * tok_rows, (1 - seq) * half_rows + places * tok_rows])
    query_start = seq * half_rows + row * tok_rows
    attn_out = attention(query, query_start, keys, values, key_start)

    states = gathered[:, 4 * HD : 4 * HD + head_rows].astype(F32).reshape(ROWS, heads, HP, NSTATE)
    logs = gathered[:, 4 * HD + head_rows :, 0].astype(F32)
    logs = logs[:, :heads] + logs[:, heads:]
    later = places[None, :] > places[:, None]
    ahead = places < row
    log_to_end = jnp.sum(jnp.where(later[:, :, None], logs[None], 0.0), axis=1)
    log_between = jnp.sum(jnp.where((later & ahead[None, :])[:, :, None], logs[None], 0.0), axis=1)
    log_ahead = jnp.sum(jnp.where(ahead[:, None], logs, 0.0), axis=0)
    half_end = jnp.sum(jnp.exp(log_to_end)[:, :, None, None] * states, axis=0)
    earlier_half = lax.ppermute(half_end.astype(BF16), "seq", [(0, 1)]).astype(F32)
    weight = jnp.where(ahead[:, None], jnp.exp(log_between), 0.0)
    prior = jnp.sum(weight[:, :, None, None] * states, axis=0)
    prior = prior + jnp.exp(log_ahead)[:, None, None] * earlier_half

    lower = position[:, None] >= position[None, :]
    inner = lax.dot_general(c_cols, b_cols, (((0,), (0,)), ((), ())), precision=HIGHEST)
    decays = jnp.exp(jnp.where(lower[None], cumulative[:, :, None] - cumulative[:, None, :], -jnp.inf))
    coefficient = inner[None] * decays * step_size[:, None, :]
    within = jnp.einsum("htu,uhp->thp", coefficient, inputs.reshape(tok_rows, heads, HP), precision=HIGHEST)
    carried = lax.dot_general(
        c_cols, prior.reshape(head_rows, NSTATE), (((0,), (1,)), ((), ())), precision=HIGHEST
    )
    result = within.reshape(tok_rows, -1) + over_heads(jnp.exp(cumulative)) * carried
    result = result + jnp.repeat(d_skip, HP)[None, :] * inputs
    gated = (result * jax.nn.silu(gate_raw)).reshape(tok_rows, heads, HP)
    normed = gated * lax.rsqrt(jnp.mean(gated * gated, axis=-1, keepdims=True) + 1e-05)
    ssm_out = normed.reshape(tok_rows, head_rows).astype(BF16)

    mixer = lax.all_gather(jnp.concatenate([attn_out, ssm_out], axis=1), "row", axis=0, tiled=True)
    w_out = jnp.concatenate([w_attn_out, w_ssm_out], axis=0)
    terms = jnp.dot(mixer, w_out, preferred_element_type=F32)
    parts = terms.astype(BF16).reshape(COLS, -1, terms.shape[1])
    swapped = lax.all_to_all(parts, "col", 0, 0, tiled=True)
    return jnp.sum(swapped.astype(F32), axis=0).astype(BF16)


def solution(mesh):
    in_specs = (
        P("seq", "row"),
        P("row", "col"),
        P("row", "col"),
        P("row", "col"),
        P("row", "col"),
        P("row", "col"),
        P("row", None),
        P("row", "col"),
        P("col"),
        P("col"),
        P("col"),
        P("col", "row"),
        P("col", "row"),
    )
    out_specs = P(("seq", "col"), "row")
    return jax.shard_map(
        on_device, mesh=mesh, in_specs=in_specs, out_specs=out_specs, check_vma=False
    )
```

```python
import jax
import jax.numpy as jnp
from jax import lax
from jax.experimental import pallas as pl
from jax.experimental.pallas import tpu as pltpu
from jax.sharding import PartitionSpec as P

HD = 128
HP = 64
NSTATE = 128
RING = 8
ROWS = 16
COLS = 8
TOK = 128
F32 = jnp.float32
BF16 = jnp.bfloat16
HIGHEST = lax.Precision.HIGHEST
VMEM_LIMIT = 48 * 1024 * 1024


def ring_step(array, step):
    return lax.ppermute(array, "row", [(i, (i + 2 * step) % ROWS) for i in range(ROWS)])


def other_core(array):
    return lax.ppermute(array, "row", [(i, i ^ 1) for i in range(ROWS)])


def after(value, *others):
    return lax.optimization_barrier((value,) + others)[0]


class Reduce:
    def __init__(self, term, wire, right_hops):
        self.term = term
        self.wire = wire
        self.limits = (right_hops, RING - 1 - right_hops)
        self.held = [None, None]
        self.sent = ()

    def hop(self, hop, *earlier):
        now = {}
        for way, sign in ((0, 1), (1, -1)):
            if hop <= self.limits[way]:
                term = self.term(sign * hop, *earlier)
                if self.held[way] is not None:
                    term = self.held[way].astype(F32) + term
                now[way] = term.astype(self.wire)
        for way, sign in ((1, -1), (0, 1)):
            if way in now:
                self.held[way] = ring_step(now[way], sign)
        self.sent = tuple(now.values())

    def result(self):
        return self.term(0) + self.held[0].astype(F32) + self.held[1].astype(F32)


def by_rows(weight, tokens):
    return lax.dot_general(weight, tokens, (((0,), (1,)), ((), ())), preferred_element_type=F32)


def nt_dot(a, b):
    return lax.dot_general(a, b, (((1,), (1,)), ((), ())), preferred_element_type=F32)


def tn_dot(a, b):
    return lax.dot_general(a, b, (((0,), (0,)), ((), ())), preferred_element_type=F32)


def scan_kernel(place_ref, ug_ref, own_ref, rate_ref, skip_ref, y_ref, state_ref, cum_ref):
    chunks, heads = own_ref.shape[0], RING
    chip = place_ref[0]
    first = own_ref.shape[2] - 2 * heads
    steps = []
    for j in range(chunks):
        rows = own_ref[j, 0, first:].astype(F32)
        mine = lax.broadcasted_iota(jnp.int32, rows.shape, 0) % heads == chip
        steps.append(jnp.sum(jnp.where(mine, rows, 0.0), axis=0, keepdims=True))
    step_all = jnp.concatenate(steps, axis=0)
    ahead = lax.broadcasted_iota(jnp.int32, (TOK, TOK), 0)
    behind = lax.broadcasted_iota(jnp.int32, (TOK, TOK), 1)
    upto = (ahead <= behind).astype(F32)
    cum_all = jnp.dot(-rate_ref[chip] * step_all, upto, precision=HIGHEST, preferred_element_type=F32)
    cum_ref[...] = cum_all
    columns = jnp.concatenate([cum_all, step_all], axis=0).T
    skip = skip_ref[chip]
    state = jnp.zeros((HP, NSTATE), F32)
    for j in range(chunks):
        raw = ug_ref[j * TOK : (j + 1) * TOK, :].T[:HP]
        inputs = raw / (1.0 + jnp.exp(-raw))
        b_cols = own_ref[j, 0, 4 * HD : 4 * HD + NSTATE]
        c_cols = own_ref[j, 0, 4 * HD + NSTATE : 4 * HD + 2 * NSTATE]
        step = step_all[j : j + 1, :]
        cum = cum_all[j : j + 1, :]
        end = cum_all[j : j + 1, TOK - 1 : TOK]
        cum_column = columns[:, j : j + 1]
        step_column = columns[:, chunks + j : chunks + j + 1]
        decay = jnp.exp(jnp.where(ahead <= behind, cum - cum_column, -1e30))
        mix = tn_dot(b_cols, c_cols) * decay * step_column
        y = jnp.dot(inputs.astype(BF16), mix.astype(BF16), preferred_element_type=F32)
        if j:
            y = y + jnp.exp(cum) * jnp.dot(state.astype(BF16), c_cols, preferred_element_type=F32)
        y_ref[j] = y + skip * inputs
        weighted = inputs * (jnp.exp(end - cum) * step)
        state = jnp.exp(end) * state + nt_dot(weighted.astype(BF16), b_cols)
    state_ref[:HP] = state
    total = jnp.sum(cum_all[:, TOK - 1 : TOK], axis=0, keepdims=True)
    state_ref[HP:] = jnp.broadcast_to(total, (8, NSTATE))


def finish_kernel(place_ref, ug_ref, own_ref, cum_ref, y_ref, state_ref, out_ref):
    state = state_ref[...].astype(BF16)
    before = jnp.zeros((1, 1), F32)
    for j in range(own_ref.shape[0]):
        gate = ug_ref[j * TOK : (j + 1) * TOK, :].T[HP:]
        cum = cum_ref[j : j + 1, :]
        c_cols = own_ref[j, 0, 4 * HD + NSTATE : 4 * HD + 2 * NSTATE]
        carried = jnp.dot(state, c_cols, preferred_element_type=F32)
        gated = (y_ref[j] + jnp.exp(cum + before) * carried) * (gate / (1.0 + jnp.exp(-gate)))
        mean = jnp.mean(gated * gated, axis=0, keepdims=True)
        out_ref[j] = (gated * lax.rsqrt(mean + 1e-05)).astype(BF16)
        before = before + cum[:, TOK - 1 : TOK]


def whole(array):
    return pl.BlockSpec(array.shape, lambda i, place: (0,) * array.ndim)


def of_core(gathered):
    return pl.BlockSpec((RING, 1) + gathered.shape[2:], lambda i, place: (0, place[1], 0, 0))


def on_core(kernel, place, gathered, before, after_own, out_shape):
    smem = pl.BlockSpec(memory_space=pltpu.SMEM)
    many = isinstance(out_shape, tuple)
    return pl.pallas_call(
        kernel,
        grid_spec=pltpu.PrefetchScalarGridSpec(
            num_scalar_prefetch=1,
            grid=(1,),
            in_specs=[whole(a) for a in before]
            + [of_core(gathered)]
            + [whole(a) if a.ndim > 1 else smem for a in after_own],
            out_specs=tuple(whole(o) for o in out_shape) if many else whole(out_shape),
        ),
        out_shape=out_shape,
        compiler_params=pltpu.CompilerParams(vmem_limit_bytes=VMEM_LIMIT),
    )(place, *before, gathered, *after_own)


def attention_kernel(place_ref, query_ref, gathered_ref, out_ref):
    group = query_ref.shape[0] // HD
    query = jnp.concatenate([query_ref[g * HD : (g + 1) * HD] for g in range(group)], axis=1)
    wide = group * TOK
    chunk = 4 * TOK
    query_start = place_ref[2]
    query_pos = query_start + lax.broadcasted_iota(jnp.int32, (1, wide), 1) % TOK

    def one(n, carry):
        other = n // 4
        core = (n // 2) % 2
        quad = n % 2
        start = place_ref[3 + other] + core * (RING * TOK) + quad * chunk

        def work(carry):
            best, total, summed = carry
            rows = pl.multiple_of(other * 2 * HD, 2 * HD)
            blocks = [(4 * quad + i, core) for i in range(4)]
            keys = jnp.concatenate([gathered_ref[z, k, pl.ds(rows, HD), :] for z, k in blocks], axis=0)
            values = jnp.concatenate([gathered_ref[z, k, pl.ds(rows + HD, HD), :] for z, k in blocks], axis=1)
            scores = jnp.dot(keys, query, preferred_element_type=F32) * HD ** (-0.5)
            key_pos = start + lax.broadcasted_iota(jnp.int32, (chunk, 1), 0)
            scores = jnp.where(key_pos <= query_pos, scores, -1e30)
            new_best = jnp.maximum(best, jnp.max(scores, axis=0, keepdims=True))
            fade = jnp.exp(best - new_best)
            weights = jnp.exp(scores - new_best).astype(BF16)
            total = total * fade + jnp.sum(weights.astype(F32), axis=0, keepdims=True)
            summed = summed * fade + jnp.dot(values, weights, preferred_element_type=F32)
            return new_best, total, summed

        return lax.cond(start < query_start + TOK, work, lambda c: c, carry)

    start = (jnp.full((1, wide), -1e30, F32), jnp.zeros((1, wide), F32), jnp.zeros((HD, wide), F32))
    _, total, summed = lax.fori_loop(0, 8, one, start)
    output = (summed / total).astype(BF16)
    for g in range(group):
        out_ref[g * HD : (g + 1) * HD] = output[:, g * TOK : (g + 1) * TOK]


def attention(place, query, gathered):
    return pl.pallas_call(
        attention_kernel,
        grid_spec=pltpu.PrefetchScalarGridSpec(
            num_scalar_prefetch=1,
            grid=(1,),
            in_specs=[whole(query), whole(gathered)],
            out_specs=whole(query),
        ),
        out_shape=jax.ShapeDtypeStruct(query.shape, BF16),
        compiler_params=pltpu.CompilerParams(vmem_limit_bytes=VMEM_LIMIT),
    )(place, query, gathered)


def heads_kernel(inputs_ref, gate_ref, out_ref):
    for h in range(inputs_ref.shape[1] // HP):
        columns = slice(h * HP, (h + 1) * HP)
        both = jnp.concatenate([inputs_ref[:, columns], gate_ref[:, columns]], axis=1)
        out_ref[:, 2 * h * HP : 2 * (h + 1) * HP] = both


def heads_together(w_inputs, w_gate):
    features, width = w_inputs.shape
    return pl.pallas_call(
        heads_kernel, out_shape=jax.ShapeDtypeStruct((features, 2 * width), BF16)
    )(w_inputs, w_gate)


def output_kernel(attn_ref, ssm_ref, w_attn_ref, w_ssm_ref, out_ref):
    attn = jnp.concatenate([attn_ref[0, 0], attn_ref[1, 0]], axis=1)
    ssm = jnp.concatenate([ssm_ref[:, 0, i].reshape(RING * HP, TOK) for i in range(2)], axis=1)
    total = jnp.dot(w_attn_ref[...], attn, preferred_element_type=F32)
    total = total + jnp.dot(w_ssm_ref[...], ssm, preferred_element_type=F32)
    half = total.shape[0] // 2
    out_ref[0] = jnp.concatenate([total[:half], total[half:]], axis=1).astype(BF16)


def output_terms(gathered, w_attn, w_ssm):
    width, attn_rows = w_attn.shape
    groups = gathered.shape[2] // HP
    by_head = gathered.reshape(RING, 2, groups, HP, TOK)
    first = attn_rows // HP // 2
    return pl.pallas_call(
        output_kernel,
        grid=(COLS,),
        in_specs=[
            pl.BlockSpec((2, 1, attn_rows, TOK), lambda b: (b % 4, b // 4, 0, 0)),
            pl.BlockSpec((RING, 1, 2, HP, TOK), lambda b: (0, b // 4, first + b % 4, 0, 0)),
            pl.BlockSpec((width, attn_rows), lambda b: (0, 0)),
            pl.BlockSpec((width, w_ssm.shape[1]), lambda b: (0, 0)),
        ],
        out_specs=pl.BlockSpec((1, width // 2, 4 * TOK), lambda b: (b, 0, 0)),
        out_shape=jax.ShapeDtypeStruct((COLS, width // 2, 4 * TOK), BF16),
        compiler_params=pltpu.CompilerParams(vmem_limit_bytes=VMEM_LIMIT),
    )(gathered, by_head, w_attn, w_ssm)


def on_device(
    hidden,
    w_query,
    w_key,
    w_value,
    w_ssm_in,
    w_gate,
    w_bc,
    w_dt,
    dt_bias,
    a_rate,
    d_skip,
    w_attn_out,
    w_ssm_out,
):
    row = lax.axis_index("row")
    seq = lax.axis_index("seq")
    chip = row // 2
    core = row % 2
    half_rows = hidden.shape[0]
    core_rows = half_rows // 2
    features = hidden.shape[1]
    heads = w_dt.shape[1]
    kv_width = w_value.shape[1]
    bc_width = w_bc.shape[1]

    kept = lax.dynamic_slice_in_dim(hidden, core * core_rows, core_rows, 0)
    sent = lax.dynamic_slice_in_dim(hidden, (1 - core) * core_rows, core_rows, 0)
    tokens = jnp.concatenate([kept, other_core(sent)], axis=1)

    def both_cores(own, axis):
        return jnp.concatenate([own, other_core(own)], axis=axis)

    def terms_of(product):
        def term(hop, *earlier):
            to_chip = (chip + hop + RING) % RING
            if earlier:
                to_chip = after(to_chip, *earlier)
            return lax.dynamic_slice_in_dim(product, to_chip * TOK, TOK, 1)

        return term

    w_first = both_cores(jnp.concatenate([w_key, w_value, w_bc, w_dt], axis=1), 0)
    first = Reduce(terms_of(by_rows(w_first, tokens)), F32, 4)
    first.hop(4)

    w_heads = both_cores(heads_together(after(w_ssm_in, *first.sent), w_gate), 0)
    third_product = jnp.dot(tokens, w_heads, preferred_element_type=F32)
    first.hop(3, *first.sent)
    w_second = both_cores(after(w_query, *first.sent), 0)
    second_product = by_rows(w_second, tokens)
    first.hop(2, *first.sent, third_product)
    first.hop(1, *first.sent, second_product)
    second = Reduce(terms_of(second_product), F32, 4)
    third = Reduce(terms_of(third_product), BF16, 3)
    second.hop(4, *first.sent)
    third.hop(4, *first.sent)
    kvbd = first.result()
    for hop in (3, 2, 1):
        third.hop(hop, *second.sent, *third.sent)
        second.hop(hop, *second.sent, *third.sent)
    ug = third.result()
    query = second.result().astype(BF16)

    key = kvbd[:kv_width].T.astype(BF16)
    value = kvbd[kv_width : 2 * kv_width].astype(BF16)
    bc_act = jax.nn.silu(kvbd[2 * kv_width : 2 * kv_width + bc_width]).astype(BF16)
    step_size = jax.nn.softplus(kvbd[2 * kv_width + bc_width :] + dt_bias[:, None])
    pair = jnp.concatenate([key, value], axis=0)
    pair_other = lax.ppermute(pair, "seq", [(0, 1), (1, 0)])
    step_high = step_size.astype(BF16)
    step_low = (step_size - step_high.astype(F32)).astype(BF16)
    message = jnp.concatenate([pair, pair_other, bc_act, step_high, step_low], axis=0)
    gathered = lax.all_gather(message, "row", axis=0, tiled=False).reshape((RING, 2) + message.shape)

    own_start = seq * half_rows
    place = jnp.stack(
        [
            chip,
            core,
            own_start + core * core_rows + chip * TOK,
            own_start,
            jnp.where(seq == 0, 1 << 20, 0),
        ]
    ).astype(jnp.int32)
    y, final, cum = on_core(
        scan_kernel,
        place,
        gathered,
        (ug,),
        (a_rate, d_skip),
        (
            jax.ShapeDtypeStruct((RING, HP, TOK), F32),
            jax.ShapeDtypeStruct((HP + 8, NSTATE), F32),
            jax.ShapeDtypeStruct((RING, TOK), F32),
        ),
    )
    theirs = other_core(final)
    early = jnp.where(core == 0, final, theirs)
    late = jnp.where(core == 0, theirs, final)
    half_end = jnp.exp(late[HP : HP + 1]) * early[:HP] + late[:HP]
    carried = jnp.where(seq == 0, 0.0, lax.ppermute(half_end, "seq", [(0, 1), (1, 0)]))
    prior = jnp.where(core == 0, carried, early[:HP] + jnp.exp(early[HP : HP + 1]) * carried)
    attn_out = attention(place, query, gathered)
    ssm_out = on_core(
        finish_kernel, place, gathered, (ug,), (cum, y, prior), jax.ShapeDtypeStruct((RING, HP, TOK), BF16)
    )

    mixer = jnp.concatenate([attn_out, ssm_out.reshape(RING * HP, TOK)], axis=0)
    mixers = lax.all_gather(mixer, "row", axis=0, tiled=False).reshape((RING, 2) + mixer.shape)
    terms = output_terms(mixers, w_attn_out.T, w_ssm_out.T)
    swapped = lax.all_to_all(terms, "col", 0, 0, tiled=True)
    mixed = jnp.sum(swapped.astype(F32), axis=0).astype(BF16)
    return jnp.concatenate([mixed[:, : 2 * TOK].T, mixed[:, 2 * TOK :].T], axis=1)


def solution(mesh):
    in_specs = (
        P("seq", "row"),
        P("row", "col"),
        P("row", "col"),
        P("row", "col"),
        P("row", "col"),
        P("row", "col"),
        P("row", None),
        P("row", "col"),
        P("col"),
        P("col"),
        P("col"),
        P("col", "row"),
        P("col", "row"),
    )
    out_specs = P(("seq", "col"), "row")
    return jax.shard_map(
        on_device, mesh=mesh, in_specs=in_specs, out_specs=out_specs, check_vma=False
    )
```

```python
import jax
import jax.numpy as jnp
from jax import lax
from jax.experimental import pallas as pl
from jax.experimental.pallas import tpu as pltpu
from jax.sharding import PartitionSpec as P

HD = 128
HP = 64
NSTATE = 128
RING = 8
ROWS = 16
COLS = 8
TOK = 128
F32 = jnp.float32
BF16 = jnp.bfloat16
HIGHEST = lax.Precision.HIGHEST
VMEM_LIMIT = 48 * 1024 * 1024


def ring_step(array, step):
    return lax.ppermute(array, "row", [(i, (i + 2 * step) % ROWS) for i in range(ROWS)])


def other_core(array):
    return lax.ppermute(array, "row", [(i, i ^ 1) for i in range(ROWS)])


def after(value, *others):
    return lax.optimization_barrier((value,) + others)[0]


class Reduce:
    def __init__(self, term, wire, right_hops):
        self.term = term
        self.wire = wire
        self.limits = (right_hops, RING - 1 - right_hops)
        self.held = [None, None]
        self.sent = ()

    def hop(self, hop, *earlier):
        now = {}
        for way, sign in ((0, 1), (1, -1)):
            if hop <= self.limits[way]:
                term = self.term(sign * hop, *earlier)
                if self.held[way] is not None:
                    term = self.held[way].astype(F32) + term
                now[way] = term.astype(self.wire)
        for way, sign in ((1, -1), (0, 1)):
            if way in now:
                self.held[way] = ring_step(now[way], sign)
        self.sent = tuple(now.values())

    def result(self):
        return self.term(0) + self.held[0].astype(F32) + self.held[1].astype(F32)


def by_rows(weight, tokens):
    return lax.dot_general(weight, tokens, (((0,), (1,)), ((), ())), preferred_element_type=F32)


def nt_dot(a, b):
    return lax.dot_general(a, b, (((1,), (1,)), ((), ())), preferred_element_type=F32)


def tn_dot(a, b):
    return lax.dot_general(a, b, (((0,), (0,)), ((), ())), preferred_element_type=F32)


def scan_kernel(place_ref, ug_ref, own_ref, rate_ref, skip_ref, y_ref, state_ref, cum_ref):
    chunks, heads = own_ref.shape[0], RING
    chip = place_ref[0]
    first = own_ref.shape[2] - 2 * heads
    steps = []
    for j in range(chunks):
        rows = own_ref[j, 0, first:].astype(F32)
        mine = lax.broadcasted_iota(jnp.int32, rows.shape, 0) % heads == chip
        steps.append(jnp.sum(jnp.where(mine, rows, 0.0), axis=0, keepdims=True))
    step_all = jnp.concatenate(steps, axis=0)
    ahead = lax.broadcasted_iota(jnp.int32, (TOK, TOK), 0)
    behind = lax.broadcasted_iota(jnp.int32, (TOK, TOK), 1)
    upto = (ahead <= behind).astype(F32)
    cum_all = jnp.dot(-rate_ref[chip] * step_all, upto, precision=HIGHEST, preferred_element_type=F32)
    cum_ref[...] = cum_all
    columns = jnp.concatenate([cum_all, step_all], axis=0).T
    skip = skip_ref[chip]
    state = jnp.zeros((HP, NSTATE), F32)
    for j in range(chunks):
        raw = ug_ref[j * TOK : (j + 1) * TOK, :].T[:HP]
        inputs = raw / (1.0 + jnp.exp(-raw))
        b_cols = own_ref[j, 0, 4 * HD : 4 * HD + NSTATE]
        c_cols = own_ref[j, 0, 4 * HD + NSTATE : 4 * HD + 2 * NSTATE]
        step = step_all[j : j + 1, :]
        cum = cum_all[j : j + 1, :]
        end = cum_all[j : j + 1, TOK - 1 : TOK]
        cum_column = columns[:, j : j + 1]
        step_column = columns[:, chunks + j : chunks + j + 1]
        decay = jnp.exp(jnp.where(ahead <= behind, cum - cum_column, -1e30))
        mix = tn_dot(b_cols, c_cols) * decay * step_column
        y = jnp.dot(inputs.astype(BF16), mix.astype(BF16), preferred_element_type=F32)
        if j:
            y = y + jnp.exp(cum) * jnp.dot(state.astype(BF16), c_cols, preferred_element_type=F32)
        y_ref[j] = y + skip * inputs
        weighted = inputs * (jnp.exp(end - cum) * step)
        state = jnp.exp(end) * state + nt_dot(weighted.astype(BF16), b_cols)
    state_ref[:HP] = state
    total = jnp.sum(cum_all[:, TOK - 1 : TOK], axis=0, keepdims=True)
    state_ref[HP:] = jnp.broadcast_to(total, (8, NSTATE))


def finish_kernel(place_ref, ug_ref, own_ref, cum_ref, y_ref, state_ref, out_ref):
    state = state_ref[...].astype(BF16)
    before = jnp.zeros((1, 1), F32)
    for j in range(own_ref.shape[0]):
        gate = ug_ref[j * TOK : (j + 1) * TOK, :].T[HP:]
        cum = cum_ref[j : j + 1, :]
        c_cols = own_ref[j, 0, 4 * HD + NSTATE : 4 * HD + 2 * NSTATE]
        carried = jnp.dot(state, c_cols, preferred_element_type=F32)
        gated = (y_ref[j] + jnp.exp(cum + before) * carried) * (gate / (1.0 + jnp.exp(-gate)))
        mean = jnp.mean(gated * gated, axis=0, keepdims=True)
        out_ref[j] = (gated * lax.rsqrt(mean + 1e-05)).astype(BF16)
        before = before + cum[:, TOK - 1 : TOK]


def whole(array):
    return pl.BlockSpec(array.shape, lambda i, place: (0,) * array.ndim)


def of_core(gathered):
    return pl.BlockSpec((RING, 1) + gathered.shape[2:], lambda i, place: (0, place[1], 0, 0))


def on_core(kernel, place, gathered, before, after_own, out_shape):
    smem = pl.BlockSpec(memory_space=pltpu.SMEM)
    many = isinstance(out_shape, tuple)
    return pl.pallas_call(
        kernel,
        grid_spec=pltpu.PrefetchScalarGridSpec(
            num_scalar_prefetch=1,
            grid=(1,),
            in_specs=[whole(a) for a in before]
            + [of_core(gathered)]
            + [whole(a) if a.ndim > 1 else smem for a in after_own],
            out_specs=tuple(whole(o) for o in out_shape) if many else whole(out_shape),
        ),
        out_shape=out_shape,
        compiler_params=pltpu.CompilerParams(vmem_limit_bytes=VMEM_LIMIT),
    )(place, *before, gathered, *after_own)


def attention_kernel(place_ref, query_ref, gathered_ref, out_ref):
    group = query_ref.shape[0] // HD
    query = jnp.concatenate([query_ref[g * HD : (g + 1) * HD] for g in range(group)], axis=1)
    wide = group * TOK
    chunk = 4 * TOK
    query_start = place_ref[2]
    query_pos = query_start + lax.broadcasted_iota(jnp.int32, (1, wide), 1) % TOK

    def one(n, carry):
        other = n // 4
        core = (n // 2) % 2
        quad = n % 2
        start = place_ref[3 + other] + core * (RING * TOK) + quad * chunk

        def work(carry):
            best, total, summed = carry
            rows = pl.multiple_of(other * 2 * HD, 2 * HD)
            blocks = [(4 * quad + i, core) for i in range(4)]
            keys = jnp.concatenate([gathered_ref[z, k, pl.ds(rows, HD), :] for z, k in blocks], axis=0)
            values = jnp.concatenate([gathered_ref[z, k, pl.ds(rows + HD, HD), :] for z, k in blocks], axis=1)
            scores = jnp.dot(keys, query, preferred_element_type=F32) * HD ** (-0.5)
            key_pos = start + lax.broadcasted_iota(jnp.int32, (chunk, 1), 0)
            scores = jnp.where(key_pos <= query_pos, scores, -1e30)
            new_best = jnp.maximum(best, jnp.max(scores, axis=0, keepdims=True))
            fade = jnp.exp(best - new_best)
            weights = jnp.exp(scores - new_best).astype(BF16)
            total = total * fade + jnp.sum(weights.astype(F32), axis=0, keepdims=True)
            summed = summed * fade + jnp.dot(values, weights, preferred_element_type=F32)
            return new_best, total, summed

        return lax.cond(start < query_start + TOK, work, lambda c: c, carry)

    start = (jnp.full((1, wide), -1e30, F32), jnp.zeros((1, wide), F32), jnp.zeros((HD, wide), F32))
    _, total, summed = lax.fori_loop(0, 8, one, start)
    output = (summed / total).astype(BF16)
    for g in range(group):
        out_ref[g * HD : (g + 1) * HD] = output[:, g * TOK : (g + 1) * TOK]


def attention(place, query, gathered):
    return pl.pallas_call(
        attention_kernel,
        grid_spec=pltpu.PrefetchScalarGridSpec(
            num_scalar_prefetch=1,
            grid=(1,),
            in_specs=[whole(query), whole(gathered)],
            out_specs=whole(query),
        ),
        out_shape=jax.ShapeDtypeStruct(query.shape, BF16),
        compiler_params=pltpu.CompilerParams(vmem_limit_bytes=VMEM_LIMIT),
    )(place, query, gathered)


def heads_kernel(inputs_ref, gate_ref, out_ref):
    for h in range(inputs_ref.shape[1] // HP):
        columns = slice(h * HP, (h + 1) * HP)
        both = jnp.concatenate([inputs_ref[:, columns], gate_ref[:, columns]], axis=1)
        out_ref[:, 2 * h * HP : 2 * (h + 1) * HP] = both


def heads_together(w_inputs, w_gate):
    features, width = w_inputs.shape
    return pl.pallas_call(
        heads_kernel, out_shape=jax.ShapeDtypeStruct((features, 2 * width), BF16)
    )(w_inputs, w_gate)


def around(array):
    return lax.ppermute(array, "row", [(i, (i + 2 - 4 * (i % 2)) % ROWS) for i in range(ROWS)])


class Gather:
    def __init__(self, block, core):
        other = other_core(block)
        self.core = core
        self.rows = block.shape[0]
        self.pair = jnp.concatenate(
            [jnp.where(core == 0, block, other), jnp.where(core == 0, other, block)], axis=0
        )
        self.found = [self.pair]
        self.sent = (self.pair,)

    def hop(self):
        self.pair = around(self.pair)
        self.sent = (self.pair,)
        self.found = self.found + [self.pair, other_core(self.pair)]

    def last(self):
        half = around(lax.dynamic_slice_in_dim(self.pair, self.core * self.rows, self.rows, 0))
        other = other_core(half)
        self.found = self.found + [half, other]


def output_kernel(place_ref, *refs):
    count = RING + 1
    found = (refs[:count], refs[count : 2 * count])
    w_attn_ref, w_ssm_ref, out_ref, attn, ssm, sems = refs[2 * count :]
    chip, core = place_ref[0], place_ref[1]
    rows = attn.shape[1] // 2
    copies = []
    for which, (blocks, held) in enumerate(zip(found, (attn, ssm))):
        for n, block in enumerate(blocks):
            distance = (n + 1) // 2
            way = (1 - 2 * core) * (1 if n % 2 == 0 else -1)
            to_chip = (chip + way * distance + RING) % RING
            if n < count - 2:
                target = held.at[to_chip]
            else:
                side = core if n == count - 2 else 1 - core
                target = held.at[to_chip, pl.ds(pl.multiple_of(side * rows, rows), rows)]
            copies.append(pltpu.make_async_copy(block, target, sems.at[which, n]))
    for copy in copies:
        copy.start()
    for copy in copies:
        copy.wait()
    for piece in range(COLS):
        k, j = piece // 4, 2 * (piece % 4)
        mine = slice(k * rows, (k + 1) * rows)
        tokens = jnp.concatenate([attn[j, mine], attn[j + 1, mine]], axis=1)
        total = jnp.dot(w_attn_ref[...], tokens, preferred_element_type=F32)
        first = k * rows + j * HP
        states = jnp.concatenate(
            [
                jnp.concatenate([ssm[z, first + i * HP : first + (i + 1) * HP] for z in range(RING)], axis=0)
                for i in range(2)
            ],
            axis=1,
        )
        total = total + jnp.dot(w_ssm_ref[...], states, preferred_element_type=F32)
        half = total.shape[0] // 2
        out_ref[piece] = jnp.concatenate([total[:half], total[half:]], axis=1).astype(BF16)


def output_terms(place, attn, ssm, w_attn, w_ssm):
    width = w_attn.shape[0]
    found = attn.found + ssm.found
    held = pltpu.VMEM((RING, 2 * attn.rows, TOK), BF16)
    out_shape = jax.ShapeDtypeStruct((COLS, width // 2, 4 * TOK), BF16)
    return pl.pallas_call(
        output_kernel,
        grid_spec=pltpu.PrefetchScalarGridSpec(
            num_scalar_prefetch=1,
            grid=(1,),
            in_specs=[pl.BlockSpec(memory_space=pl.ANY)] * len(found) + [whole(w_attn), whole(w_ssm)],
            out_specs=whole(out_shape),
            scratch_shapes=[held, held, pltpu.SemaphoreType.DMA((2, RING + 1))],
        ),
        out_shape=out_shape,
        compiler_params=pltpu.CompilerParams(vmem_limit_bytes=VMEM_LIMIT),
    )(place, *found, w_attn, w_ssm)


def on_device(
    hidden,
    w_query,
    w_key,
    w_value,
    w_ssm_in,
    w_gate,
    w_bc,
    w_dt,
    dt_bias,
    a_rate,
    d_skip,
    w_attn_out,
    w_ssm_out,
):
    row = lax.axis_index("row")
    seq = lax.axis_index("seq")
    chip = row // 2
    core = row % 2
    half_rows = hidden.shape[0]
    core_rows = half_rows // 2
    features = hidden.shape[1]
    heads = w_dt.shape[1]
    kv_width = w_value.shape[1]
    bc_width = w_bc.shape[1]

    kept = lax.dynamic_slice_in_dim(hidden, core * core_rows, core_rows, 0)
    sent = lax.dynamic_slice_in_dim(hidden, (1 - core) * core_rows, core_rows, 0)
    tokens = jnp.concatenate([kept, other_core(sent)], axis=1)

    def both_cores(own, axis):
        return jnp.concatenate([own, other_core(own)], axis=axis)

    def terms_of(product):
        def term(hop, *earlier):
            to_chip = (chip + hop + RING) % RING
            if earlier:
                to_chip = after(to_chip, *earlier)
            return lax.dynamic_slice_in_dim(product, to_chip * TOK, TOK, 1)

        return term

    w_first = both_cores(jnp.concatenate([w_key, w_value, w_bc, w_dt], axis=1), 0)
    first = Reduce(terms_of(by_rows(w_first, tokens)), F32, 4)
    first.hop(4)

    w_heads = both_cores(heads_together(after(w_ssm_in, *first.sent), w_gate), 0)
    third_product = jnp.dot(tokens, w_heads, preferred_element_type=F32)
    first.hop(3, *first.sent)
    w_second = both_cores(after(w_query, *first.sent), 0)
    second_product = by_rows(w_second, tokens)
    first.hop(2, *first.sent, third_product)
    first.hop(1, *first.sent, second_product)
    second = Reduce(terms_of(second_product), F32, 4)
    third = Reduce(terms_of(third_product), BF16, 3)
    second.hop(4, *first.sent)
    third.hop(4, *first.sent)
    kvbd = first.result()
    for hop in (3, 2, 1):
        third.hop(hop, *second.sent, *third.sent)
        second.hop(hop, *second.sent, *third.sent)
    ug = third.result()
    query = second.result().astype(BF16)

    key = kvbd[:kv_width].T.astype(BF16)
    value = kvbd[kv_width : 2 * kv_width].astype(BF16)
    bc_act = jax.nn.silu(kvbd[2 * kv_width : 2 * kv_width + bc_width]).astype(BF16)
    step_size = jax.nn.softplus(kvbd[2 * kv_width + bc_width :] + dt_bias[:, None])
    pair = jnp.concatenate([key, value], axis=0)
    pair_other = lax.ppermute(pair, "seq", [(0, 1), (1, 0)])
    step_high = step_size.astype(BF16)
    step_low = (step_size - step_high.astype(F32)).astype(BF16)
    message = jnp.concatenate([pair, pair_other, bc_act, step_high, step_low], axis=0)
    gathered = lax.all_gather(message, "row", axis=0, tiled=False).reshape((RING, 2) + message.shape)

    own_start = seq * half_rows
    place = jnp.stack(
        [
            chip,
            core,
            own_start + core * core_rows + chip * TOK,
            own_start,
            jnp.where(seq == 0, 1 << 20, 0),
        ]
    ).astype(jnp.int32)
    y, final, cum = on_core(
        scan_kernel,
        place,
        gathered,
        (ug,),
        (a_rate, d_skip),
        (
            jax.ShapeDtypeStruct((RING, HP, TOK), F32),
            jax.ShapeDtypeStruct((HP + 8, NSTATE), F32),
            jax.ShapeDtypeStruct((RING, TOK), F32),
        ),
    )
    theirs = other_core(final)
    early = jnp.where(core == 0, final, theirs)
    late = jnp.where(core == 0, theirs, final)
    half_end = jnp.exp(late[HP : HP + 1]) * early[:HP] + late[:HP]
    carried = jnp.where(seq == 0, 0.0, lax.ppermute(half_end, "seq", [(0, 1), (1, 0)]))
    prior = jnp.where(core == 0, carried, early[:HP] + jnp.exp(early[HP : HP + 1]) * carried)
    attn = Gather(attention(place, query, gathered), core)
    attn.hop()
    ssm_out = on_core(
        finish_kernel, place, gathered, (ug,), (cum, y, prior), jax.ShapeDtypeStruct((RING, HP, TOK), BF16)
    )
    ssm = Gather(ssm_out.reshape(RING * HP, TOK), core)

    ssm.hop()
    attn.hop()
    ssm.hop()
    attn.hop()
    ssm.hop()
    attn.last()
    ssm.last()
    terms = output_terms(place, attn, ssm, w_attn_out.T, w_ssm_out.T)
    swapped = lax.all_to_all(terms, "col", 0, 0, tiled=True)
    mixed = jnp.sum(swapped.astype(F32), axis=0).astype(BF16)
    return jnp.concatenate([mixed[:, : 2 * TOK].T, mixed[:, 2 * TOK :].T], axis=1)


def solution(mesh):
    in_specs = (
        P("seq", "row"),
        P("row", "col"),
        P("row", "col"),
        P("row", "col"),
        P("row", "col"),
        P("row", "col"),
        P("row", None),
        P("row", "col"),
        P("col"),
        P("col"),
        P("col"),
        P("col", "row"),
        P("col", "row"),
    )
    out_specs = P(("seq", "col"), "row")
    return jax.shard_map(
        on_device, mesh=mesh, in_specs=in_specs, out_specs=out_specs, check_vma=False
    )
```
